128 devices in a mesh: section: 16 (over x, z_hi, core), fsdp: 8 (over z_lo, y).
Axes of the slice: x: 4, y: 4, z: 4 (z_hi: 2, z_lo: 2; z = z_hi * 2 + z_lo), core: 2. Of those that a mesh axis runs over, the one named last changes fastest.
Arguments:
- x_in: bfloat16 [2, 16, 512, 3072], P(None, 'section', 'fsdp'), may hold values from -6 to 6
- expert_ids: int32 [2, 16, 512, 2], P(None, 'section', 'fsdp'), may hold values from 0 to 3, all different within a row; in each aligned block of 64 rows (0 to 63, 64 to 127, ..., all dimensions but the last counted through in order) at most 48 rows name the same one
- out_grad: bfloat16 [2, 16, 512, 3072], P(None, 'section', 'fsdp'), may hold values from -6 to 6
- norm_gain: float32 [2, 16, 3072], P(None, 'section'), may hold values from 0.25 to 1.75
- router: bfloat16 [2, 16, 3072, 4], P(None, 'section'), may hold values from -0.109375 to 0.109375
- w_gate: bfloat16 [2, 16, 3072, 3072], P(None, 'section', None, 'fsdp'), may hold values from -0.109375 to 0.109375
- w_up: bfloat16 [2, 16, 3072, 3072], P(None, 'section', None, 'fsdp'), may hold values from -0.109375 to 0.109375
- w_down: bfloat16 [2, 16, 3072, 3072], P(None, 'section', 'fsdp'), may hold values from -0.21875 to 0.21875
Outputs:
- next_fwd: bfloat16 [2, 16, 512, 3072], P(None, 'section', 'fsdp')
- prev_grad: bfloat16 [2, 16, 512, 3072], P(None, 'section', 'fsdp')
- grad_gate: bfloat16 [16, 3072, 3072], P('section', None, 'fsdp')
- grad_up: bfloat16 [16, 3072, 3072], P('section', None, 'fsdp')
- grad_down: bfloat16 [16, 3072, 3072], P('section', 'fsdp')
- grad_router: bfloat16 [16, 3072, 4], P('section')
The draws below stay inside these ranges and needn't reach their ends.
Inputs may be any that keep to these rules, and one draw needn't show every extreme that they name: `expert_ids`: the two experts of a token differ. Within one aligned block of 64 rows (one micro-batch's tokens on one device), no expert is named more than 48 times, a bound that some block reaches.
All inputs are finite; a program needn't handle non-finite values.
Results may differ from the reference program's by a relative error of at most 0.024.
Values may be sent and summed in bfloat16 or wider, within the bound.
No kernel may reach another device: no remote copies, remote signals or barrier semaphores. Data moves between devices by JAX's collectives and lax.ppermute only.
A program may use at most 128 MiB of HBM per device.

```python
import math
import jax
import jax.numpy as jnp
import numpy as np
from jax import lax

D = 3072
EXPERTS = 4
FF_DEV = 384
TOK_DEV = 64
SECTIONS = 16
SPLIT = 2
FF = 768
TOKENS = 512
CAP = 48
N_FSDP = 8


def shard_levels(rng, dims, shards, smallest, high):
    level = 1.0
    for dim, shards_of in shards:
        steps = jax.random.uniform(jax.random.fold_in(jax.random.fold_in(rng, 6), dim), (shards_of,), jnp.float32, smallest / len(shards), high / len(shards))
        level = level * jnp.repeat(jnp.exp(steps), dims[dim] // shards_of).reshape((-1,) + (1,) * (len(dims) - 1 - dim))
    return level


def assign_block(own_key, own, number, rows, amount, top, limit, slope):
    ranking = jax.random.permutation(own_key, amount)
    heavy_load, common = load_shares(amount, rows * top, limit, slope, True), load_shares(amount, rows * top, limit, slope, False)
    places = jnp.arange(amount)

    def named(lengths, offset_by):
        used = int((lengths > 0).sum())
        fixed = max(1, used // 4)
        shifted = fixed + (places - fixed + offset_by * (used - fixed)) % max(1, amount - fixed)
        return jnp.zeros((amount,), jnp.int32).at[ranking[jnp.where(places < fixed, places, shifted)]].set(jnp.asarray(lengths, jnp.int32))

    lengths = jnp.where(number % 4 == 0, named(heavy_load, number // 4), named(common, number - number // 4 - 1))
    mixed = jax.random.permutation(jax.random.fold_in(own, 3), amount)
    giver, taker = mixed[0:amount // 2 * 2:2], mixed[1:amount // 2 * 2:2]
    room = jnp.minimum(lengths[giver] - 1, limit - lengths[taker]) // 2
    room = jnp.where((giver == ranking[0]) | (taker == ranking[0]) | (lengths[taker] == 0), 0, jnp.maximum(room, 0))
    shifted = jax.random.randint(jax.random.fold_in(own, 4), (amount // 2,), 0, 1 << 20) % (room + 1)
    lengths = lengths.at[giver].add(-shifted).at[taker].add(shifted)
    labels = jnp.searchsorted(jnp.cumsum(lengths), jnp.arange(rows * top), side="right").astype(jnp.int32)
    table = labels.reshape(top, rows).T
    table = table[jax.random.permutation(jax.random.fold_in(own, 1), rows)]
    offset_by = jax.random.randint(jax.random.fold_in(own, 2), (rows, 1), 0, top)
    return jnp.take_along_axis(table, (jnp.arange(top)[None, :] + offset_by) % top, axis=1)


def load_shares(amount, total, reach, lean, full):
    portions = [(1 << 20) // math.isqrt(grade ** lean) + 1 for grade in range(1, amount + 1)]
    largest = reach if full else min(reach, max(-(-total // amount), total * portions[0] // sum(portions)))
    least = 1 if total - largest >= amount - 1 else 0
    given, rest = [largest] + [least] * (amount - 1), total - largest - least * (amount - 1)
    while rest > 0:
        movable = [i for i in range(1, amount) if given[i] < largest] or [i for i in range(1, amount) if given[i] < reach]
        pool, left = sum([portions[i] for i in movable]), rest
        for i in movable:
            more = min(reach - given[i], max(1, left * portions[i] // pool), rest)
            given[i] = given[i] + more
            rest = rest - more
    return np.array(given)


def noise(stream_key, shape, width, limit, cuts=(), kind=jnp.bfloat16):
    level = shard_levels(stream_key, shape, cuts, -0.22, 0.18) if cuts else 1.0
    result = jax.random.normal(stream_key, shape, jnp.float32) * width * level
    return jnp.minimum(jnp.maximum(result, -limit), limit).astype(kind)


def setup_inputs(seed: int = 0) -> dict:
    key_list = jax.random.split(jax.random.key(seed), 9)
    x_in = noise(key_list[0], (2, SECTIONS, TOKENS, D), 1.0, 6.0, ((1, 16), (2, 8)))
    expert_ids_keys = jax.random.split(jax.random.fold_in(key_list[1], 1), 2 * SECTIONS * TOKENS // TOK_DEV)
    expert_ids_turns = jax.random.permutation(jax.random.fold_in(key_list[1], 3), 2 * SECTIONS * TOKENS // TOK_DEV)
    expert_ids = jax.vmap(lambda own, number: assign_block(jax.random.fold_in(key_list[1], 2), own, number, TOK_DEV, EXPERTS, 2, CAP, 1))(expert_ids_keys, expert_ids_turns).reshape((2, SECTIONS, TOKENS, 2))
    out_grad = noise(key_list[2], (2, SECTIONS, TOKENS, D), 1.0, 6.0, ((1, 16), (2, 8)))
    norm_gain = jnp.clip(1.0 + 0.15 * jax.random.normal(key_list[3], (2, SECTIONS, D), jnp.float32), 0.25, 1.75)
    router = noise(key_list[4], (2, SECTIONS, D, EXPERTS), D ** -0.5, 0.109375, ((1, 16),))
    w_gate = noise(key_list[5], (2, SECTIONS, D, EXPERTS * FF), D ** -0.5, 0.109375, ((1, 16), (3, 8)))
    w_up = noise(key_list[6], (2, SECTIONS, D, EXPERTS * FF), D ** -0.5, 0.109375, ((1, 16), (3, 8)))
    w_down = noise(key_list[7], (2, SECTIONS, EXPERTS * FF, D), FF ** -0.5, 0.21875, ((1, 16), (2, 8)))
    return dict(x_in=x_in, expert_ids=expert_ids, out_grad=out_grad, norm_gain=norm_gain, router=router, w_gate=w_gate, w_up=w_up, w_down=w_down)


EPSILON = 1e-05

def normalize(values, scales):
    factor = lax.rsqrt(lax.optimization_barrier(jnp.mean(values * values, axis=-1, keepdims=True)) + EPSILON)
    return values * factor * scales

def routing(picks, experts, capacity):
    count_rows = picks.shape[1]
    expert_lanes = jnp.arange(experts, dtype=jnp.int32)
    first_pick = (picks[..., 0:1] == expert_lanes).astype(jnp.float32)
    second_pick = (picks[..., 1:2] == expert_lanes).astype(jnp.float32)
    row_index = jnp.arange(count_rows, dtype=jnp.int32)
    before = (row_index[None, :] < row_index[:, None]).astype(jnp.float32)
    earlier = jnp.einsum('tu,bue->bte', before, first_pick + second_pick)
    offsets = earlier + capacity * expert_lanes.astype(jnp.float32)
    first_slot = lax.optimization_barrier(jnp.sum(first_pick * offsets, axis=-1))
    second_slot = lax.optimization_barrier(jnp.sum(second_pick * offsets, axis=-1))
    slot_lanes = jnp.arange(experts * capacity, dtype=jnp.int32).astype(jnp.float32)
    first_place = (slot_lanes[None, :, None] == first_slot[:, None, :]).astype(jnp.float32)
    second_place = (slot_lanes[None, :, None] == second_slot[:, None, :]).astype(jnp.float32)
    return (first_pick, second_pick, first_place, second_place)

def to_experts(blocks_data):
    return blocks_data.reshape(N_FSDP, EXPERTS, CAP, D).transpose(1, 0, 2, 3).reshape(EXPERTS, N_FSDP * CAP, D)

def to_blocks(expert_data):
    return expert_data.reshape(EXPERTS, N_FSDP, CAP, D).transpose(1, 0, 2, 3).reshape(N_FSDP, EXPERTS * CAP, D)

def section_pass(operands):
    section_rows, picks, upstream, scales, mixer, gate_mat, up_mat, down_mat = operands
    wide = jnp.float32
    inputs_wide = section_rows.reshape(N_FSDP, TOK_DEV, D).astype(wide)
    picks = picks.reshape(N_FSDP, TOK_DEV, 2)
    upstream_wide = upstream.reshape(N_FSDP, TOK_DEV, D).astype(wide)
    first_pick, second_pick, first_place, second_place = routing(picks, EXPERTS, CAP)
    both_place = first_place + second_place
    normed = normalize(inputs_wide, scales).astype(jnp.bfloat16)
    normed_wide = normed.astype(wide)
    mixer_wide = mixer.astype(wide)
    logits = jnp.einsum('btd,de->bte', normed_wide, mixer_wide)
    first_weight = jax.nn.sigmoid(lax.optimization_barrier(jnp.sum((first_pick - second_pick) * logits, axis=-1)))
    second_weight = 1.0 - first_weight
    outgoing = jnp.einsum('bst,btd->bsd', both_place, normed_wide).astype(jnp.bfloat16)
    arrived = to_experts(outgoing).astype(wide)
    slot_total = arrived.shape[1]
    gate_wide = gate_mat.astype(wide).reshape(D, EXPERTS, FF).transpose(1, 0, 2)
    up_wide = up_mat.astype(wide).reshape(D, EXPERTS, FF).transpose(1, 0, 2)
    down_wide = down_mat.astype(wide).reshape(EXPERTS, FF, D)
    gate_pre = jnp.einsum('esd,edf->esf', arrived, gate_wide)
    up_pre = jnp.einsum('esd,edf->esf', arrived, up_wide)
    sigmoid_gate = jax.nn.sigmoid(gate_pre)
    activated = gate_pre * sigmoid_gate
    hidden = (activated * up_pre).astype(jnp.bfloat16).astype(wide)
    hidden_parts = hidden.reshape(EXPERTS, slot_total, SPLIT, FF_DEV)
    down_parts = down_wide.reshape(EXPERTS, SPLIT, FF_DEV, D)
    part_out = jnp.einsum('eshf,ehfd->ehsd', hidden_parts, down_parts).astype(jnp.bfloat16).astype(wide)
    expert_out = lax.optimization_barrier(jnp.sum(part_out, axis=1))
    returned = to_blocks(expert_out)
    first_out = jnp.einsum('bst,bsd->btd', first_place, returned)
    second_out = jnp.einsum('bst,bsd->btd', second_place, returned)
    section_out = (inputs_wide + first_weight[..., None] * first_out + second_weight[..., None] * second_out).astype(jnp.bfloat16)
    slot_weight = jnp.einsum('bst,bt->bs', first_place, first_weight) + jnp.einsum('bst,bt->bs', second_place, second_weight)
    picked = jnp.einsum('bst,btd->bsd', both_place, upstream_wide)
    expert_grad = (picked * slot_weight[..., None]).astype(jnp.bfloat16)
    grad_arrived = to_experts(expert_grad).astype(wide)
    hidden_grad = jnp.einsum('esd,efd->esf', grad_arrived, down_wide)
    gate_slope = sigmoid_gate * (1.0 + gate_pre * (1.0 - sigmoid_gate))
    gate_pre_grad = (hidden_grad * up_pre * gate_slope).astype(jnp.bfloat16).astype(wide)
    up_pre_grad = (hidden_grad * activated).astype(jnp.bfloat16).astype(wide)
    down_total = jnp.einsum('esf,esd->efd', hidden, grad_arrived).reshape(EXPERTS * FF, D)
    gate_total = jnp.einsum('esd,esf->edf', arrived, gate_pre_grad).transpose(1, 0, 2).reshape(D, EXPERTS * FF)
    up_total = jnp.einsum('esd,esf->edf', arrived, up_pre_grad).transpose(1, 0, 2).reshape(D, EXPERTS * FF)
    gate_grad_parts = gate_pre_grad.reshape(EXPERTS, slot_total, SPLIT, FF_DEV)
    up_grad_parts = up_pre_grad.reshape(EXPERTS, slot_total, SPLIT, FF_DEV)
    gate_parts = gate_wide.reshape(EXPERTS, D, SPLIT, FF_DEV)
    up_parts = up_wide.reshape(EXPERTS, D, SPLIT, FF_DEV)
    part_normed = (jnp.einsum('eshf,edhf->ehsd', gate_grad_parts, gate_parts) + jnp.einsum('eshf,edhf->ehsd', up_grad_parts, up_parts)).astype(jnp.bfloat16).astype(wide)
    normed_back = to_blocks(lax.optimization_barrier(jnp.sum(part_normed, axis=1)))
    normed_grad = jnp.einsum('bst,bsd->btd', both_place, normed_back)
    first_dot = lax.optimization_barrier(jnp.sum(upstream_wide * first_out, axis=-1))
    second_dot = lax.optimization_barrier(jnp.sum(upstream_wide * second_out, axis=-1))
    logit_grad = (first_dot - second_dot) * first_weight * second_weight
    logits_grad = ((first_pick - second_pick) * logit_grad[..., None]).astype(jnp.bfloat16).astype(wide)
    normed_grad = normed_grad + jnp.einsum('bte,de->btd', logits_grad, mixer_wide)
    router_total = jnp.einsum('btd,bte->de', normed_wide, logits_grad)
    _, pullback = jax.vjp(lambda values: normalize(values, scales), inputs_wide)
    input_grad = (upstream_wide + pullback(normed_grad)[0]).astype(jnp.bfloat16)
    return (section_out.reshape(TOKENS, D), input_grad.reshape(TOKENS, D), gate_total.astype(jnp.bfloat16), up_total.astype(jnp.bfloat16), down_total.astype(jnp.bfloat16), router_total.astype(jnp.bfloat16))

def mirror_sum(pair):
    own, other = lax.optimization_barrier(pair)
    return (own.astype(jnp.float32) + other[::-1].astype(jnp.float32)).astype(jnp.bfloat16)

def reference(x_in, expert_ids, out_grad, norm_gain, router, w_gate, w_up, w_down):
    results = []
    for replica in range(2):
        results.append(lax.map(section_pass, (x_in[replica], expert_ids[replica], out_grad[replica], norm_gain[replica], router[replica], w_gate[replica], w_up[replica], w_down[replica])))
    down_res, up_res = results
    next_fwd = jnp.stack([jnp.roll(down_res[0], 1, axis=0), jnp.roll(up_res[0], -1, axis=0)])
    prev_grad = jnp.stack([jnp.roll(down_res[1], -1, axis=0), jnp.roll(up_res[1], 1, axis=0)])
    grad_gate = mirror_sum((down_res[2], up_res[2]))
    grad_up = mirror_sum((down_res[3], up_res[3]))
    grad_down = mirror_sum((down_res[4], up_res[4]))
    grad_router = mirror_sum((down_res[5], up_res[5]))
    return (next_fwd, prev_grad, grad_gate, grad_up, grad_down, grad_router)
```

```python
import jax
import jax.numpy as jnp
from jax import lax
from jax.sharding import PartitionSpec as P

EPSILON = 1e-05
RING = 4
BF16 = jnp.bfloat16
F32 = jnp.float32


def permuted(value, axis, target):
    pairs = [(source, target(source)) for source in range(lax.axis_size(axis))]
    return lax.ppermute(value, axis, pairs)


def shifted(value, steps):
    count = lax.axis_size("section")
    return permuted(value, "section", lambda s: (s + steps) % count)


def mirrored(value):
    count = lax.axis_size("section")
    return permuted(value, "section", lambda s: count - 1 - s)


def ring(value, steps):
    return permuted(value, "fsdp", lambda s: s // RING * RING + (s + steps) % RING)


def across(value):
    return permuted(value, "fsdp", lambda s: s ^ RING)


def flipped(value, mask):
    return permuted(value, "fsdp", lambda s: s ^ mask)


def add_half(first, second):
    return (first.astype(F32) + second.astype(F32)).astype(BF16)


def gather_rows(own):
    half = own.shape[0]
    pair = jnp.concatenate([own, across(own)])
    from_left = ring(pair, 1)
    from_right = ring(pair, -1)
    far_own = ring(from_left[:half], 1)
    far_other = ring(from_right[half:], -1)
    return jnp.concatenate([pair, from_left, from_right, far_own, far_other])


def scatter_rows(partial):
    half = partial.shape[0] // 8
    mine, left, right, far = [partial[2 * half * i : 2 * half * (i + 1)] for i in range(4)]
    far_own = ring(far[:half], 1)
    far_other = ring(far[half:], -1)
    right = jnp.concatenate([add_half(right[:half], far_own), right[half:]])
    left = jnp.concatenate([left[:half], add_half(left[half:], far_other)])
    from_left = ring(right, 1)
    from_right = ring(left, -1)
    total = mine.astype(F32) + from_left.astype(F32) + from_right.astype(F32)
    return total[:half] + across(total[half:].astype(BF16)).astype(F32)


def gather_small(own):
    pair = jnp.stack([own, across(own)])
    near = flipped(pair, 1)
    quad = jnp.stack([pair, near])
    far = flipped(quad, 2)
    odd = lax.axis_index("fsdp") % 2 == 1
    before = jnp.where(odd, near, far[1])
    after = jnp.where(odd, far[1], near)
    return jnp.concatenate([pair, before, after, far[0]])


def sum_small(own):
    for mask in (RING, 1, 2):
        own = own + flipped(own, mask)
    return own


def normalize(values, scales):
    factor = lax.rsqrt(jnp.mean(values * values, axis=-1, keepdims=True) + EPSILON)
    return values * factor * scales


def dot(first, second, contract):
    return lax.dot_general(first, second, (contract, ((), ())), preferred_element_type=F32)


def on_device(x_in, expert_ids, out_grad, norm_gain, router, w_gate, w_up, w_down):
    experts = router.shape[3]
    sharers = lax.axis_size("fsdp") // experts
    my_expert = (jnp.arange(experts) == lax.axis_index("fsdp") // sharers).astype(F32)

    normed, extras = [], []
    for c in range(2):
        picks = expert_ids[c, 0]
        lanes = jnp.arange(experts, dtype=jnp.int32)
        first_pick = (picks[:, 0:1] == lanes).astype(F32)
        second_pick = (picks[:, 1:2] == lanes).astype(F32)
        sign = first_pick - second_pick
        rows = normalize(x_in[c, 0].astype(F32), norm_gain[c, 0]).astype(BF16)
        logits = dot(rows, router[c, 0], ((1,), (0,)))
        first_weight = jax.nn.sigmoid(jnp.sum(sign * logits, axis=-1, keepdims=True))
        second_weight = 1.0 - first_weight
        weights = first_pick * first_weight + second_pick * second_weight
        slopes = first_weight * second_weight * sign
        normed.append(rows)
        extras.append(jnp.concatenate([weights.T, sign.T, slopes.T]))
    extras = gather_small(jnp.stack(extras))

    outs, backs, pre_grads, downs, routers, rows_all = {}, {}, {}, {}, {}, {}
    for c in (1, 0):
        upstream = gather_rows(out_grad[c, 0])
        rows = gather_rows(normed[c])
        rows_all[c] = rows
        small = extras[:, c].transpose(0, 2, 1).reshape(-1, 3 * experts)
        weight = jnp.sum(small[:, :experts] * my_expert, axis=-1, keepdims=True)
        sign = small[:, experts : 2 * experts]
        slope = jnp.sum(small[:, 2 * experts :] * my_expert, axis=-1, keepdims=True)
        gate_mat, up_mat, down_mat = w_gate[c, 0], w_up[c, 0], w_down[c, 0]
        gate_pre = dot(rows, gate_mat, ((1,), (0,)))
        up_pre = dot(rows, up_mat, ((1,), (0,)))
        sigmoid_gate = jax.nn.sigmoid(gate_pre)
        activated = gate_pre * sigmoid_gate
        hidden = (activated * up_pre).astype(BF16)
        raw_grad = dot(upstream, down_mat, ((1,), (1,)))
        outs[c] = (dot(hidden, down_mat, ((1,), (0,))) * weight).astype(BF16)
        gate_slope = sigmoid_gate * (1.0 + gate_pre * (1.0 - sigmoid_gate))
        hidden_grad = raw_grad * weight
        gate_grad = (hidden_grad * up_pre * gate_slope).astype(BF16)
        up_grad = (hidden_grad * activated).astype(BF16)
        pre_grads[c] = (gate_grad, up_grad)
        weight_grad = jnp.sum(hidden.astype(F32) * raw_grad, axis=-1, keepdims=True)
        logits_grad = (sign * (slope * weight_grad)).astype(BF16)
        backs[c] = (
            dot(gate_grad, gate_mat, ((1,), (1,)))
            + dot(up_grad, up_mat, ((1,), (1,)))
            + dot(logits_grad, router[c, 0], ((1,), (1,)))
        ).astype(BF16)
        weighted_hidden = (hidden.astype(F32) * weight).astype(BF16)
        downs[c] = dot(weighted_hidden, upstream, ((0,), (0,)))
        routers[c] = dot(logits_grad, rows, ((0,), (0,)))

    next_fwd, prev_grad = {}, {}
    for c, way in ((1, -1), (0, 1)):
        inputs_wide = x_in[c, 0].astype(F32)
        section_out = (inputs_wide + scatter_rows(outs[c])).astype(BF16)
        next_fwd[c] = shifted(section_out, way)
        normed_grad = scatter_rows(backs[c])
        _, pullback = jax.vjp(lambda values: normalize(values, norm_gain[c, 0]), inputs_wide)
        input_grad = (out_grad[c, 0].astype(F32) + pullback(normed_grad)[0]).astype(BF16)
        prev_grad[c] = shifted(input_grad, -way)

    far_rows = gather_rows(mirrored(normed[1]))
    far_gate, far_up = mirrored(pre_grads[1][0]), mirrored(pre_grads[1][1])
    far_down = mirrored(downs[1].astype(BF16))

    def both(own, other):
        return (lax.reduce_precision(own, 8, 7) + lax.reduce_precision(other.astype(F32), 8, 7)).astype(BF16)

    grad_gate = both(dot(rows_all[0], pre_grads[0][0], ((0,), (0,))), dot(far_rows, far_gate, ((0,), (0,))))
    grad_up = both(dot(rows_all[0], pre_grads[0][1], ((0,), (0,))), dot(far_rows, far_up, ((0,), (0,))))
    grad_down = both(downs[0], far_down)
    router_sums = sum_small(jnp.concatenate([routers[0], routers[1]]))
    far_router = mirrored(router_sums[experts:].astype(BF16))
    grad_router = both(router_sums[:experts], far_router).T
    return (
        jnp.stack([next_fwd[0], next_fwd[1]])[:, None],
        jnp.stack([prev_grad[0], prev_grad[1]])[:, None],
        grad_gate[None],
        grad_up[None],
        grad_down[None],
        grad_router[None],
    )


def solution(mesh):
    in_specs = (
        P(None, "section", "fsdp", None),
        P(None, "section", "fsdp", None),
        P(None, "section", "fsdp", None),
        P(None, "section", None),
        P(None, "section", None, None),
        P(None, "section", None, "fsdp"),
        P(None, "section", None, "fsdp"),
        P(None, "section", "fsdp", None),
    )
    out_specs = (
        P(None, "section", "fsdp", None),
        P(None, "section", "fsdp", None),
        P("section", None, "fsdp"),
        P("section", None, "fsdp"),
        P("section", "fsdp", None),
        P("section", None, None),
    )
    return jax.shard_map(
        on_device, mesh=mesh, in_specs=in_specs, out_specs=out_specs, check_vma=False
    )
```

```python
import jax
import jax.numpy as jnp
from jax import lax
from jax.sharding import PartitionSpec as P

EPSILON = 1e-05
RING = 4
BF16 = jnp.bfloat16
F32 = jnp.float32


def permuted(value, axis, target):
    pairs = [(source, target(source)) for source in range(lax.axis_size(axis))]
    return lax.ppermute(value, axis, pairs)


def shifted(value, steps):
    count = lax.axis_size("section")
    return permuted(value, "section", lambda s: (s + steps) % count)


def mirrored(value):
    count = lax.axis_size("section")
    return permuted(value, "section", lambda s: count - 1 - s)


def ring(value, steps):
    return permuted(value, "fsdp", lambda s: s // RING * RING + (s + steps) % RING)


def across(value):
    return permuted(value, "fsdp", lambda s: s ^ RING)


def flipped(value, mask):
    return permuted(value, "fsdp", lambda s: s ^ mask)


def add_half(first, second):
    return (first.astype(F32) + second.astype(F32)).astype(BF16)


def after(value, *earlier):
    return lax.optimization_barrier((value, *earlier))[0]


def pair_rows(own):
    return jnp.concatenate([own, across(own)])


def near_rows(pair):
    return ring(pair, 1), ring(pair, -1)


def far_rows(near):
    half = near[0].shape[0] // 2
    return ring(near[0][:half], 1), ring(near[1][half:], -1)


def all_rows(pair, near, far):
    return jnp.concatenate([pair, *near, *far])


def far_sums(partial):
    half = partial.shape[0] // 8
    far = partial[6 * half :]
    return ring(far[:half], 1), ring(far[half:], -1)


def near_sums(partial, far):
    half = partial.shape[0] // 8
    left, right = partial[2 * half : 4 * half], partial[4 * half : 6 * half]
    right = jnp.concatenate([add_half(right[:half], far[0]), right[half:]])
    left = jnp.concatenate([left[:half], add_half(left[half:], far[1])])
    return ring(right, 1), ring(left, -1)


def pair_sums(partial, near):
    half = partial.shape[0] // 8
    total = partial[: 2 * half].astype(F32) + near[0].astype(F32) + near[1].astype(F32)
    return total[:half], across(total[half:].astype(BF16))


def packed(values, width):
    flat = values.reshape(-1)
    first = lax.reduce_precision(flat, 8, 7)
    second = lax.reduce_precision(flat - first, 8, 7)
    terms = jnp.stack([first, second, flat - first - second]).astype(BF16).reshape(-1)
    rows = -(-terms.shape[0] // width)
    rows = -(-rows // 8) * 8
    return jnp.pad(terms, (0, rows * width - terms.shape[0])).reshape(rows, width)


def unpacked(rows, shape):
    count = 1
    for size in shape:
        count *= size
    terms = rows.reshape(8, -1)[:, : 3 * count].reshape(8, 3, count).astype(F32)
    return jnp.sum(terms, axis=1).reshape(8, *shape)


def sum_small(own):
    for mask in (RING, 1, 2):
        own = own + flipped(own, mask)
    return own


def normalize(values, scales):
    factor = lax.rsqrt(jnp.mean(values * values, axis=-1, keepdims=True) + EPSILON)
    return values * factor * scales


def dot(first, second, contract):
    return lax.dot_general(first, second, (contract, ((), ())), preferred_element_type=F32)


def on_device(x_in, expert_ids, out_grad, norm_gain, router, w_gate, w_up, w_down):
    experts = router.shape[3]
    sharers = lax.axis_size("fsdp") // experts
    my_expert = (jnp.arange(experts) == lax.axis_index("fsdp") // sharers).astype(F32)

    normed, extras = [], []
    for c in range(2):
        picks = expert_ids[c, 0]
        lanes = jnp.arange(experts, dtype=jnp.int32)
        first_pick = (picks[:, 0:1] == lanes).astype(F32)
        second_pick = (picks[:, 1:2] == lanes).astype(F32)
        sign = first_pick - second_pick
        rows = normalize(x_in[c, 0].astype(F32), norm_gain[c, 0]).astype(BF16)
        logits = dot(rows, router[c, 0], ((1,), (0,)))
        first_weight = jax.nn.sigmoid(jnp.sum(sign * logits, axis=-1, keepdims=True))
        second_weight = 1.0 - first_weight
        weights = first_pick * first_weight + second_pick * second_weight
        slopes = first_weight * second_weight * sign
        normed.append(rows)
        extras.append(jnp.concatenate([weights.T, sign.T, slopes.T]))
    extras = jnp.stack(extras)
    small_rows = packed(extras, x_in.shape[3])

    outs, backs, pre_grads, downs, routers, rows_all, partials = {}, {}, {}, {}, {}, {}, {}

    def experts_pass(c, rows, upstream, gathered):
        rows_all[c] = rows
        small = gathered[:, c].transpose(0, 2, 1).reshape(-1, 3 * experts)
        weight = jnp.sum(small[:, :experts] * my_expert, axis=-1, keepdims=True)
        sign = small[:, experts : 2 * experts]
        slope = jnp.sum(small[:, 2 * experts :] * my_expert, axis=-1, keepdims=True)
        gate_mat, up_mat, down_mat = w_gate[c, 0], w_up[c, 0], w_down[c, 0]
        gate_pre = dot(rows, gate_mat, ((1,), (0,)))
        up_pre = dot(rows, up_mat, ((1,), (0,)))
        sigmoid_gate = jax.nn.sigmoid(gate_pre)
        activated = gate_pre * sigmoid_gate
        hidden = (activated * up_pre).astype(BF16)
        raw_grad = dot(upstream, down_mat, ((1,), (1,)))
        outs = (dot(hidden, down_mat, ((1,), (0,))) * weight).astype(BF16)
        gate_slope = sigmoid_gate * (1.0 + gate_pre * (1.0 - sigmoid_gate))
        hidden_grad = raw_grad * weight
        gate_grad = (hidden_grad * up_pre * gate_slope).astype(BF16)
        up_grad = (hidden_grad * activated).astype(BF16)
        pre_grads[c] = (gate_grad, up_grad)
        weight_grad = jnp.sum(hidden.astype(F32) * raw_grad, axis=-1, keepdims=True)
        logits_grad = (sign * (slope * weight_grad)).astype(BF16)
        backs = (
            dot(gate_grad, gate_mat, ((1,), (1,)))
            + dot(up_grad, up_mat, ((1,), (1,)))
            + dot(logits_grad, router[c, 0], ((1,), (1,)))
        ).astype(BF16)
        weighted_hidden = (hidden.astype(F32) * weight).astype(BF16)
        downs[c] = dot(weighted_hidden, upstream, ((0,), (0,)))
        routers[c] = dot(logits_grad, rows, ((0,), (0,)))
        return outs, backs

    next_fwd, prev_grad = {}, {}

    def finish_out(c, way, kept, arrived):
        section_out = (x_in[c, 0].astype(F32) + kept + arrived.astype(F32)).astype(BF16)
        next_fwd[c] = shifted(section_out, way)

    def finish_back(c, way, kept, arrived):
        normed_grad = kept + arrived.astype(F32)
        inputs_wide = x_in[c, 0].astype(F32)
        _, pullback = jax.vjp(lambda values: normalize(values, norm_gain[c, 0]), inputs_wide)
        input_grad = (out_grad[c, 0].astype(F32) + pullback(normed_grad)[0]).astype(BF16)
        prev_grad[c] = shifted(input_grad, way)

    scope = jax.named_scope
    count = out_grad.shape[2]
    with scope("zO1"):
        pair_o1 = pair_rows(out_grad[1, 0])
    with scope("zN1"):
        pair_n1 = pair_rows(jnp.concatenate([normed[1], small_rows]))
    with scope("nO1"):
        near_o1 = near_rows(pair_o1)
    with scope("nN1"):
        near_n1 = near_rows(pair_n1)
    with scope("zO0"):
        pair_o0 = pair_rows(after(out_grad[0, 0], pair_n1))
    with scope("zN0"):
        pair_n0 = pair_rows(after(normed[0], pair_n1))
    with scope("fO1"):
        far_o1 = far_rows(near_o1)
    with scope("fN1"):
        far_n1 = far_rows(near_n1)
    with scope("mN"):
        mirror_rows = mirrored(after(normed[1], pair_n0))
    with scope("nO0"):
        near_o0 = near_rows(after(pair_o0, *far_o1))
    with scope("nN0"):
        near_n0 = near_rows(after(pair_n0, *far_n1))
    with scope("zM"):
        pair_m = pair_rows(mirror_rows)
    with scope("pass1"):
        rows_n1 = all_rows(pair_n1, near_n1, far_n1).reshape(8, -1, x_in.shape[3])
        gathered = unpacked(rows_n1[:, count:], extras.shape)
        out1, back1 = experts_pass(
            1, rows_n1[:, :count].reshape(8 * count, -1), all_rows(pair_o1, near_o1, far_o1), gathered
        )
    with scope("mdown"):
        far_down = mirrored(downs[1].astype(BF16))
    with scope("mpre"):
        far_gate, far_up = mirrored(pre_grads[1][0]), mirrored(pre_grads[1][1])
    with scope("fO0"):
        far_o0 = far_rows(near_o0)
    with scope("fN0"):
        far_n0 = far_rows(near_n0)
    with scope("sfout1"):
        sfar_out1 = far_sums(after(out1, *far_o0))
    with scope("sfback1"):
        sfar_back1 = far_sums(after(back1, *far_n0))
    with scope("pass0"):
        out0, back0 = experts_pass(
            0, all_rows(pair_n0, near_n0, far_n0), all_rows(pair_o0, near_o0, far_o0), gathered
        )
    with scope("snout1"):
        snear_out1 = near_sums(out1, sfar_out1)
    with scope("snback1"):
        snear_back1 = near_sums(back1, sfar_back1)
    with scope("sfout0"):
        sfar_out0 = far_sums(after(out0, *sfar_back1))
    with scope("sfback0"):
        sfar_back0 = far_sums(after(back0, *sfar_back1))
    with scope("szout1"):
        kept_out1, arrived_out1 = pair_sums(out1, snear_out1)
    with scope("szback1"):
        kept_back1, arrived_back1 = pair_sums(back1, snear_back1)
    with scope("snout0"):
        snear_out0 = near_sums(out0, after(sfar_out0, far_down))
    with scope("snback0"):
        snear_back0 = near_sums(back0, sfar_back0)
    with scope("endout1"):
        finish_out(1, -1, kept_out1, arrived_out1)
    with scope("endback1"):
        finish_back(1, 1, kept_back1, arrived_back1)
    with scope("nM"):
        near_m = near_rows(after(pair_m, *sfar_back0))
    with scope("router"):
        router_sums = sum_small(after(jnp.concatenate([routers[0], routers[1]]), *sfar_back0))
        far_router = mirrored(router_sums[experts:].astype(BF16))
    with scope("szout0"):
        kept_out0, arrived_out0 = pair_sums(out0, snear_out0)
    with scope("szback0"):
        kept_back0, arrived_back0 = pair_sums(back0, snear_back0)
    with scope("fM"):
        far_m = far_rows(after(near_m, *snear_out0, far_gate, far_up))
    with scope("endout0"):
        finish_out(0, 1, kept_out0, arrived_out0)
    with scope("endback0"):
        finish_back(0, -1, kept_back0, arrived_back0)
    far_rows_all = all_rows(pair_m, near_m, far_m)

    def both(own, other):
        return (lax.reduce_precision(own, 8, 7) + lax.reduce_precision(other.astype(F32), 8, 7)).astype(BF16)

    grad_gate = both(dot(rows_all[0], pre_grads[0][0], ((0,), (0,))), dot(far_rows_all, far_gate, ((0,), (0,))))
    grad_up = both(dot(rows_all[0], pre_grads[0][1], ((0,), (0,))), dot(far_rows_all, far_up, ((0,), (0,))))
    grad_down = both(downs[0], far_down)
    grad_router = both(router_sums[:experts], far_router).T
    return (
        jnp.stack([next_fwd[0], next_fwd[1]])[:, None],
        jnp.stack([prev_grad[0], prev_grad[1]])[:, None],
        grad_gate[None],
        grad_up[None],
        grad_down[None],
        grad_router[None],
    )


def solution(mesh):
    in_specs = (
        P(None, "section", "fsdp", None),
        P(None, "section", "fsdp", None),
        P(None, "section", "fsdp", None),
        P(None, "section", None),
        P(None, "section", None, None),
        P(None, "section", None, "fsdp"),
        P(None, "section", None, "fsdp"),
        P(None, "section", "fsdp", None),
    )
    out_specs = (
        P(None, "section", "fsdp", None),
        P(None, "section", "fsdp", None),
        P("section", None, "fsdp"),
        P("section", None, "fsdp"),
        P("section", "fsdp", None),
        P("section", None, None),
    )
    return jax.shard_map(
        on_device, mesh=mesh, in_specs=in_specs, out_specs=out_specs, check_vma=False
    )
```

```python
import jax
import jax.numpy as jnp
from jax import lax
from jax.experimental import pallas as pl
from jax.experimental.pallas import tpu as pltpu
from jax.sharding import PartitionSpec as P

EPSILON = 1e-05
RING = 4
BF16 = jnp.bfloat16
F32 = jnp.float32
COST = 20_000_000_000


def permuted(value, axis, target):
    pairs = [(source, target(source)) for source in range(lax.axis_size(axis))]
    return lax.ppermute(value, axis, pairs)


def shifted(value, steps):
    count = lax.axis_size("section")
    return permuted(value, "section", lambda s: (s + steps) % count)


def mirrored(value):
    count = lax.axis_size("section")
    return permuted(value, "section", lambda s: count - 1 - s)


def ring(value, steps):
    return permuted(value, "fsdp", lambda s: s // RING * RING + (s + steps) % RING)


def across(value):
    return permuted(value, "fsdp", lambda s: s ^ RING)


def flipped(value, mask):
    return permuted(value, "fsdp", lambda s: s ^ mask)


def add_half(first, second):
    return (first.astype(F32) + second.astype(F32)).astype(BF16)


def after(value, *earlier):
    return lax.optimization_barrier((value, *earlier))[0]


def pair_rows(own, count):
    other = across(own)
    parts = [own[:count], other[:count], own[count:], other[count:]]
    return jnp.concatenate(parts if own.shape[0] > count else parts[:2])


def near_rows(pair):
    return ring(pair, 1), ring(pair, -1)


def far_rows(near, count):
    def part(rows, z):
        extra = (rows.shape[0] - 2 * count) // 2
        first, second = z * count, 2 * count + z * extra
        kept = rows[first : first + count]
        return jnp.concatenate([kept, rows[second : second + extra]]) if extra else kept

    low, high = lax.optimization_barrier((part(near[0], 0), part(near[1], 1)))
    return ring(low, 1), ring(high, -1)


def all_rows(pieces, count):
    return jnp.concatenate([piece[: 2 * count] for piece in pieces[:3]] + [piece[:count] for piece in pieces[3:]])


def extra_rows(pieces, count):
    return jnp.concatenate([piece[2 * count :] for piece in pieces[:3]] + [piece[count:] for piece in pieces[3:]])


def far_sums(far):
    return ring(far[0], 1), ring(far[1], -1)


def near_sums(left, right, far):
    half = left.shape[0] // 2
    right = jnp.concatenate([add_half(right[:half], far[0]), right[half:]])
    left = jnp.concatenate([left[:half], add_half(left[half:], far[1])])
    right, left = lax.optimization_barrier((right, left))
    return ring(right, 1), ring(left, -1)


def pair_sums(own, near):
    half = own.shape[0] // 2
    total = own.astype(F32) + near[0].astype(F32) + near[1].astype(F32)
    return total[:half], across(total[half:].astype(BF16))


def packed(values, width):
    flat = jnp.pad(values.reshape(-1), (0, width - values.size))
    first = lax.reduce_precision(flat, 8, 7)
    second = lax.reduce_precision(flat - first, 8, 7)
    terms = jnp.stack([first, second, flat - first - second]).astype(BF16)
    return jnp.pad(terms, ((0, 5), (0, 0)))


def unpacked(rows):
    terms = rows.reshape(8, 8, -1).astype(F32)
    return (terms[:, 0] + terms[:, 1] + terms[:, 2]).reshape(8, -1, 128)


def normalize(values, scales):
    factor = lax.rsqrt(jnp.mean(values * values, axis=-1, keepdims=True) + EPSILON)
    return values * factor * scales


def dot(first, second, contract):
    return lax.dot_general(first, second, (contract, ((), ())), preferred_element_type=F32)


def in_places(refs, count):
    if len(refs) == 5:
        each = [(refs, 2 * count, 0), (refs, 2 * count, count)]
    else:
        each = [(refs[:-5], count, 0), (refs[-5:], count, 0)]
    result = []
    for mine, step, first in each:
        if len(mine) == 8:
            result.append([(ref, 0) for ref in mine])
        else:
            result.append([(mine[k // 2], k % 2 * step + first) for k in range(6)] + [(mine[3], first), (mine[4], first)])
    return result


def out_places(refs, count, merged):
    result = []
    for which in range(2):
        near = refs[2:5] if merged else refs[2 + 3 * which : 5 + 3 * which]
        step, first = (2 * count, which * count) if merged else (count, 0)
        far = [(refs[i], which * count) for i in range(2)]
        result.append([(near[k // 2], k % 2 * step + first) for k in range(6)] + far)
    return result


def experts_kernel(c, experts, count, taken, out_merged, *refs):
    small_ref, mine_ref, router_ref = refs[:3]
    refs = refs[3:]
    up_blocks, row_blocks = in_places(refs[:taken], count)
    mats, refs = refs[taken : taken + 3], refs[taken + 3 :]
    taken = 5 if out_merged else 8
    out_blocks, back_blocks = out_places(refs[:taken], count, out_merged)
    refs = refs[taken:]
    down_out_ref, refs = refs[0], refs[1:]
    if not out_merged:
        router_out_ref, pre_out_ref, rows_out_ref = refs[:3]
        refs = refs[3:]
    rows_ref, upstream_ref, gate_ref, up_ref, down_ref, hidden_ref, pre_grad_ref, logits_ref = refs[:8]
    turned_ref, turned_logits_ref, weight_ref, small_rows_ref, sems = refs[8:]
    units = gate_ref.shape[1]

    def copies(blocks, whole, base):
        return [
            pltpu.make_async_copy(ref.at[pl.ds(first, count)], whole.at[pl.ds(count * k, count)], sems.at[base + k])
            for k, (ref, first) in enumerate(blocks)
        ]

    row_copies = copies(row_blocks, rows_ref, 0)
    up_copies = copies(up_blocks, upstream_ref, 8)
    mat_copies = [
        pltpu.make_async_copy(mat.at[c, 0], whole, sems.at[16 + i])
        for i, (mat, whole) in enumerate(zip(mats, (gate_ref, up_ref, down_ref)))
    ]
    for copy in row_copies + mat_copies[:2] + up_copies + mat_copies[2:]:
        copy.start()
    mine = mine_ref[...]
    blank = jnp.zeros((128 - small_ref.shape[1], 128), F32)
    for i in range(8):
        block = jnp.concatenate([small_ref[i], blank], axis=0).T
        small_rows_ref[count * i : count * (i + 1), :] = block[c * count : (c + 1) * count, :]
    for copy in row_copies + mat_copies[:2]:
        copy.wait()
    if not out_merged:
        rows_out = pltpu.make_async_copy(rows_ref, rows_out_ref, sems.at[19])
        rows_out.start()
    for copy in up_copies + mat_copies[2:]:
        copy.wait()
    block = 4 * count

    def rows_step(i, carry):
        span = pl.ds(pl.multiple_of(i * block, block), block)
        small = small_rows_ref[span, :]
        weight = jnp.sum(small * mine[0:1, :], axis=-1, keepdims=True)
        slope = jnp.sum(small * mine[1:2, :], axis=-1, keepdims=True)
        gate_pre = dot(rows_ref[span, :], gate_ref[...], ((1,), (0,)))
        up_pre = dot(rows_ref[span, :], up_ref[...], ((1,), (0,)))
        raw_grad = dot(upstream_ref[span, :], down_ref[...], ((1,), (1,)))
        sigmoid_gate = jax.nn.sigmoid(gate_pre)
        activated = gate_pre * sigmoid_gate
        hidden = (activated * up_pre).astype(BF16)
        hidden_wide = hidden.astype(F32)
        weight_grad = jnp.sum(hidden_wide * raw_grad, axis=-1, keepdims=True)
        hidden_grad = raw_grad * weight
        gate_slope = sigmoid_gate * (1.0 + gate_pre * (1.0 - sigmoid_gate))
        pre_grad_ref[span, :units] = (hidden_grad * up_pre * gate_slope).astype(BF16)
        pre_grad_ref[span, units:] = (hidden_grad * activated).astype(BF16)
        logits_grad = (small * mine[2:3, :] * (slope * weight_grad)).astype(BF16)
        logits_ref[span, :] = logits_grad
        turned_logits_ref[i] = logits_grad.astype(F32).T[:8]
        hidden_ref[span, :] = hidden
        weight_ref[span, :] = jnp.broadcast_to(weight, (block, 128))
        turned_ref[i] = (hidden_wide * weight).T.astype(BF16)
        return carry

    lax.fori_loop(0, 2, rows_step, 0)
    width = rows_ref.shape[1]
    total = 8 * count
    if out_merged:
        each = width // (2 * units)
        for i in range(each):
            part = pre_grad_ref[i * (total // each) : (i + 1) * (total // each), :]
            down_out_ref[units : units + total // each, i * 2 * units : (i + 1) * 2 * units] = part
    else:
        pre_out_ref[...] = pre_grad_ref[...]
    chunk = 512 if width % 512 == 0 else 128

    def columns_step(i, carry):
        span = pl.ds(pl.multiple_of(i * chunk, chunk), chunk)
        out = (dot(hidden_ref[...], down_ref[:, span], ((1,), (0,))) * weight_ref[:, 0:1]).astype(BF16)
        back = (
            dot(pre_grad_ref[:, :units], gate_ref[span, :], ((1,), (1,)))
            + dot(pre_grad_ref[:, units:], up_ref[span, :], ((1,), (1,)))
            + dot(logits_ref[...], router_ref[:, span], ((1,), (0,)))
        ).astype(BF16)
        for blocks, value in ((out_blocks, out), (back_blocks, back)):
            for k, (ref, first) in enumerate(blocks):
                ref[first : first + count, span] = value[count * k : count * (k + 1)]
        router_sum = dot(
            turned_logits_ref[0].astype(BF16), rows_ref[:block, span], ((1,), (0,))
        ) + dot(turned_logits_ref[1].astype(BF16), rows_ref[block:, span], ((1,), (0,)))
        if out_merged:
            high = router_sum.astype(BF16).astype(F32)
            both = jnp.concatenate([high, router_sum - high]).astype(BF16)
            down_out_ref[down_out_ref.shape[0] - 16 :, span] = both
        else:
            router_out_ref[:, span] = router_sum
        down_out_ref[:units, span] = (
            dot(turned_ref[0], upstream_ref[:block, span], ((1,), (0,)))
            + dot(turned_ref[1], upstream_ref[block:, span], ((1,), (0,)))
        ).astype(BF16)
        return carry

    lax.fori_loop(0, width // chunk, columns_step, 0)
    if not out_merged:
        rows_out.wait()


def experts_call(c, experts, count, small, mine, router_rows, pieces, mats, out_merged):
    width, units = mats[0].shape[2:]
    total = 8 * count
    full = pl.BlockSpec(memory_space=pltpu.VMEM)
    hbm = pl.BlockSpec(memory_space=pl.ANY)
    shape = lambda rows, columns: jax.ShapeDtypeStruct((rows, columns), BF16)
    near = 4 * count if out_merged else 2 * count
    results = [shape(2 * count, width)] * 2 + [shape(near, width)] * (3 if out_merged else 6)
    results.append(shape(units + total * 2 * units // width + 16 if out_merged else units, width))
    specs = [full] * len(results)
    if not out_merged:
        results += [jax.ShapeDtypeStruct((8, width), F32), shape(total, 2 * units), shape(total, width)]
        specs += [full, full, hbm]
    return pl.pallas_call(
        lambda *refs: experts_kernel(c, experts, count, len(pieces), out_merged, *refs),
        in_specs=[full] * 3 + [hbm] * (len(pieces) + 3),
        out_specs=specs,
        out_shape=results,
        scratch_shapes=[
            pltpu.VMEM((total, width), BF16),
            pltpu.VMEM((total, width), BF16),
            pltpu.VMEM((width, units), BF16),
            pltpu.VMEM((width, units), BF16),
            pltpu.VMEM((units, width), BF16),
            pltpu.VMEM((total, units), BF16),
            pltpu.VMEM((total, 2 * units), BF16),
            pltpu.VMEM((total, 128), BF16),
            pltpu.VMEM((2, units, total // 2), BF16),
            pltpu.VMEM((2, 8, total // 2), F32),
            pltpu.VMEM((total, 128), F32),
            pltpu.VMEM((total, 128), F32),
            pltpu.SemaphoreType.DMA((20,)),
        ],
        compiler_params=pltpu.CompilerParams(vmem_limit_bytes=48 * 1024 * 1024),
        cost_estimate=pl.CostEstimate(flops=COST, bytes_accessed=20_000_000, transcendentals=0),
        name=f"experts{c}",
    )(small, mine, router_rows, *pieces, *mats)


def on_device(x_in, expert_ids, out_grad, norm_gain, router, w_gate, w_up, w_down):
    experts = router.shape[3]
    count, units = out_grad.shape[2], w_gate.shape[3]
    sharers = lax.axis_size("fsdp") // experts
    lane = jnp.arange(128)
    expert = lax.axis_index("fsdp") // sharers
    mine = jnp.stack(
        [lane == expert, lane == 2 * experts + expert, lane // experts == 1] + [lane < 0] * 5
    ).astype(F32)

    normed, extras = [], []
    for c in range(2):
        picks = expert_ids[c, 0]
        lanes = jnp.arange(experts, dtype=jnp.int32)
        first_pick = (picks[:, 0:1] == lanes).astype(F32)
        second_pick = (picks[:, 1:2] == lanes).astype(F32)
        sign = first_pick - second_pick
        rows = normalize(x_in[c, 0].astype(F32), norm_gain[c, 0]).astype(BF16)
        logits = dot(rows, router[c, 0], ((1,), (0,)))
        first_weight = jax.nn.sigmoid(jnp.sum(sign * logits, axis=-1, keepdims=True))
        second_weight = 1.0 - first_weight
        weights = first_pick * first_weight + second_pick * second_weight
        slopes = first_weight * second_weight * sign
        normed.append(rows)
        extras.append(jnp.concatenate([weights.T, sign.T, slopes.T]))
    small_rows = packed(jnp.concatenate(extras, axis=1), x_in.shape[3])

    def experts_pass(c, pieces, small, out_merged):
        router_rows = jnp.pad(router[c, 0].T, ((experts, 128 - 2 * experts), (0, 0)))
        return experts_call(
            c, experts, count, small, mine, router_rows, pieces, (w_gate, w_up, w_down), out_merged
        )

    next_fwd, prev_grad = {}, {}

    def finish_out(c, way, kept, arrived):
        section_out = (x_in[c, 0].astype(F32) + kept + arrived.astype(F32)).astype(BF16)
        next_fwd[c] = shifted(section_out, way)

    def finish_back(c, way, kept, arrived):
        normed_grad = kept + arrived.astype(F32)
        inputs_wide = x_in[c, 0].astype(F32)
        _, pullback = jax.vjp(lambda values: normalize(values, norm_gain[c, 0]), inputs_wide)
        input_grad = (out_grad[c, 0].astype(F32) + pullback(normed_grad)[0]).astype(BF16)
        prev_grad[c] = shifted(input_grad, way)

    scope = jax.named_scope
    own_o1 = out_grad[1, 0]
    with scope("nO1own"):
        near_own = ring(own_o1, 1), ring(own_o1, -1)
    with scope("zO1"):
        other_o1 = across(own_o1)
    with scope("zN1"):
        pair_n1 = pair_rows(after(jnp.concatenate([normed[1], small_rows]), other_o1), count)
    with scope("nO1other"):
        near_other = ring(other_o1, 1), ring(other_o1, -1)
    with scope("fO1"):
        low, high, *_ = lax.optimization_barrier((near_own[0], near_other[1], near_own[1], near_other[0]))
        far_o1 = ring(low, 1), ring(high, -1)
    with scope("nN1"):
        near_n1 = near_rows(after(pair_n1, *near_other))
    with scope("z0"):
        pair_0 = pair_rows(after(jnp.concatenate([out_grad[0, 0], normed[0]]), pair_n1), 2 * count)
    with scope("fN1"):
        far_n1 = far_rows(near_n1, count)
    with scope("n0"):
        near_0 = near_rows(after(pair_0, *far_o1, *far_n1))
    with scope("mN"):
        mirror_rows = mirrored(after(normed[1], pair_0))
    with scope("zM"):
        pair_m = pair_rows(after(mirror_rows, *far_n1), count)
    with scope("pass1"):
        pieces_n1 = (pair_n1, *near_n1, *far_n1)
        small = unpacked(extra_rows(after(pieces_n1, pair_0), count))
        blocks_o1 = (own_o1, other_o1, near_own[0], near_other[0], near_own[1], near_other[1], *far_o1)
        *far1, own1, left1, right1, mirror1 = experts_pass(1, blocks_o1 + pieces_n1, small, True)
    with scope("s1"):
        sfar_1 = far_sums(far1)
    with scope("m1"):
        mirror_grads = mirrored(mirror1)
    with scope("f0"):
        far_0 = far_rows(after(near_0, *sfar_1), 2 * count)
    with scope("t1"):
        snear_1 = near_sums(left1, right1, sfar_1)
    with scope("pass0"):
        *far0, own_o, left_o, right_o, own_b, left_b, right_b, down0, router0, pre0, rows0 = experts_pass(
            0, (pair_0, *near_0, *far_0), small, False
        )
    with scope("s0"):
        sfar_0 = far_sums(far0)
    with scope("rz"):
        first_row = mirror_grads.shape[0] - 16
        router_terms = mirror_grads[first_row:].astype(F32)
        routers = jnp.concatenate([router0[experts:], router_terms[experts : 2 * experts] + router_terms[3 * experts :]])
        routers = routers + flipped(routers, RING)
        high = lax.reduce_precision(routers, 8, 7)
        router_rows = jnp.concatenate([high, routers - high]).astype(BF16)
    with scope("tback0"):
        snear_b = near_sums(*after((left_b, right_b), router_rows), (sfar_0[0][count:], sfar_0[1][count:]))
    with scope("z1"):
        kept_1, arrived_1 = pair_sums(own1, snear_1)
    with scope("tout0"):
        snear_o = near_sums(left_o, right_o, (sfar_0[0][:count], sfar_0[1][:count]))
    with scope("end1"):
        finish_out(1, -1, kept_1[:count], arrived_1[:count])
        finish_back(1, 1, kept_1[count:], arrived_1[count:])
    with scope("nM"):
        near_m = near_rows(after(jnp.concatenate([pair_m, router_rows]), *snear_b))
    with scope("zback0"):
        kept_b, arrived_b = pair_sums(after(own_b, arrived_1), snear_b)
    with scope("zout0"):
        kept_o, arrived_o = pair_sums(after(own_o, next_fwd[1], prev_grad[1]), snear_o)
    with scope("fM"):
        low, high = near_m[0], near_m[1][count : 2 * count]
        low = jnp.concatenate([low[:count], low[2 * count :]])
        low, high = lax.optimization_barrier((low, high))
        far_m = ring(low, 1), ring(high, -1)
    with scope("endback0"):
        finish_back(0, -1, kept_b, arrived_b)
    with scope("endout0"):
        finish_out(0, 1, kept_o, arrived_o)
    far_rows_all = all_rows((pair_m, *near_m, *far_m), count)
    router_parts = [router_rows, near_m[0][2 * count :], near_m[1][2 * count :], far_m[0][count:]]
    routers = sum(part.astype(F32) for part in router_parts)
    routers = routers[: 2 * experts] + routers[2 * experts :]

    def both(own, other):
        return (lax.reduce_precision(own, 8, 7) + lax.reduce_precision(other.astype(F32), 8, 7)).astype(BF16)

    far_pre = mirror_grads[units:first_row]
    far_pre = jnp.concatenate(jnp.split(far_pre, far_pre.shape[1] // (2 * units), axis=1))

    def weight_grad(first):
        span = slice(first, first + units)
        own = lax.optimization_barrier(dot(rows0, pre0[:, span], ((0,), (0,))).astype(BF16))
        return both(own.astype(F32), dot(far_rows_all, far_pre[:, span], ((0,), (0,))))

    grad_gate, grad_up = weight_grad(0), weight_grad(units)
    grad_down = both(down0.astype(F32), mirror_grads[:units])
    grad_router = both(routers[:experts], routers[experts:]).T
    return (
        jnp.stack([next_fwd[0], next_fwd[1]])[:, None],
        jnp.stack([prev_grad[0], prev_grad[1]])[:, None],
        grad_gate[None],
        grad_up[None],
        grad_down[None],
        grad_router[None],
    )


def solution(mesh):
    in_specs = (
        P(None, "section", "fsdp", None),
        P(None, "section", "fsdp", None),
        P(None, "section", "fsdp", None),
        P(None, "section", None),
        P(None, "section", None, None),
        P(None, "section", None, "fsdp"),
        P(None, "section", None, "fsdp"),
        P(None, "section", "fsdp", None),
    )
    out_specs = (
        P(None, "section", "fsdp", None),
        P(None, "section", "fsdp", None),
        P("section", None, "fsdp"),
        P("section", None, "fsdp"),
        P("section", "fsdp", None),
        P("section", None, None),
    )
    return jax.shard_map(
        on_device, mesh=mesh, in_specs=in_specs, out_specs=out_specs, check_vma=False
    )
```

```python
import jax
import jax.numpy as jnp
from jax import lax
from jax.experimental import pallas as pl
from jax.experimental.pallas import tpu as pltpu
from jax.sharding import PartitionSpec as P

EPSILON = 1e-05
RING = 4
BF16 = jnp.bfloat16
F32 = jnp.float32
COST = 20_000_000_000


def permuted(value, axis, target):
    pairs = [(source, target(source)) for source in range(lax.axis_size(axis))]
    return lax.ppermute(value, axis, pairs)


def shifted(value, steps):
    count = lax.axis_size("section")
    return permuted(value, "section", lambda s: (s + steps) % count)


def mirrored(value):
    count = lax.axis_size("section")
    return permuted(value, "section", lambda s: count - 1 - s)


def ring(value, steps):
    return permuted(value, "fsdp", lambda s: s // RING * RING + (s + steps) % RING)


def across(value):
    return permuted(value, "fsdp", lambda s: s ^ RING)


def flipped(value, mask):
    return permuted(value, "fsdp", lambda s: s ^ mask)


def add_half(first, second):
    return (first.astype(F32) + second.astype(F32)).astype(BF16)


def after(value, *earlier):
    return lax.optimization_barrier((value, *earlier))[0]


def pair_rows(own, count):
    other = across(own)
    parts = [own[:count], other[:count], own[count:], other[count:]]
    return jnp.concatenate(parts if own.shape[0] > count else parts[:2])


def near_rows(pair):
    return ring(pair, 1), ring(pair, -1)


def far_rows(near, count):
    def part(rows, z):
        extra = (rows.shape[0] - 2 * count) // 2
        first, second = z * count, 2 * count + z * extra
        kept = rows[first : first + count]
        return jnp.concatenate([kept, rows[second : second + extra]]) if extra else kept

    low, high = lax.optimization_barrier((part(near[0], 0), part(near[1], 1)))
    return ring(low, 1), ring(high, -1)


def all_rows(pieces, count):
    return jnp.concatenate([piece[: 2 * count] for piece in pieces[:3]] + [piece[:count] for piece in pieces[3:]])


def extra_rows(pieces, count):
    return jnp.concatenate([piece[2 * count :] for piece in pieces[:3]] + [piece[count:] for piece in pieces[3:]])


def far_sums(far):
    return ring(far[0], 1), ring(far[1], -1)


def near_sums(left, right, far):
    half = left.shape[0] // 2
    right = jnp.concatenate([add_half(right[:half], far[0]), right[half:]])
    left = jnp.concatenate([left[:half], add_half(left[half:], far[1])])
    right, left = lax.optimization_barrier((right, left))
    return ring(right, 1), ring(left, -1)


def pair_sums(own, near):
    half = own.shape[0] // 2
    total = own.astype(F32) + near[0].astype(F32) + near[1].astype(F32)
    return total[:half], across(total[half:].astype(BF16))


def packed(values, width):
    flat = jnp.pad(values.reshape(-1), (0, width - values.size))
    first = lax.reduce_precision(flat, 8, 7)
    second = lax.reduce_precision(flat - first, 8, 7)
    terms = jnp.stack([first, second, flat - first - second]).astype(BF16)
    return jnp.pad(terms, ((0, 5), (0, 0)))


def unpacked(rows):
    terms = rows.reshape(8, 8, -1).astype(F32)
    return (terms[:, 0] + terms[:, 1] + terms[:, 2]).reshape(8, -1, 128)


def normalize(values, scales):
    factor = lax.rsqrt(jnp.mean(values * values, axis=-1, keepdims=True) + EPSILON)
    return values * factor * scales


def dot(first, second, contract):
    return lax.dot_general(first, second, (contract, ((), ())), preferred_element_type=F32)


def in_places(refs, count):
    if len(refs) == 5:
        each = [(refs, 2 * count, 0), (refs, 2 * count, count)]
    else:
        each = [(refs[:-5], count, 0), (refs[-5:], count, 0)]
    result = []
    for mine, step, first in each:
        if len(mine) == 8:
            result.append([(ref, 0) for ref in mine])
        else:
            result.append([(mine[k // 2], k % 2 * step + first) for k in range(6)] + [(mine[3], first), (mine[4], first)])
    return result


def out_places(refs, count, merged):
    result = []
    for which in range(2):
        near = refs[2:5] if merged else refs[2 + 3 * which : 5 + 3 * which]
        step, first = (2 * count, which * count) if merged else (count, 0)
        far = [(refs[i], which * count) for i in range(2)]
        result.append([(near[k // 2], k % 2 * step + first) for k in range(6)] + far)
    return result


def experts_kernel(c, experts, count, taken, out_merged, *refs):
    small_ref, mine_ref, router_ref = refs[:3]
    refs = refs[3:]
    up_blocks, row_blocks = in_places(refs[:taken], count)
    mats, refs = refs[taken : taken + 3], refs[taken + 3 :]
    taken = 5 if out_merged else 8
    out_blocks, back_blocks = out_places(refs[:taken], count, out_merged)
    refs = refs[taken:]
    down_out_ref, refs = refs[0], refs[1:]
    if not out_merged:
        router_out_ref, pre_out_ref, rows_out_ref = refs[:3]
        refs = refs[3:]
    rows_ref, upstream_ref, gate_ref, up_ref, down_ref, hidden_ref, pre_grad_ref, logits_ref = refs[:8]
    turned_ref, turned_logits_ref, weight_ref, small_rows_ref, sems = refs[8:]
    units = gate_ref.shape[1]

    def copies(blocks, whole, base):
        return [
            pltpu.make_async_copy(ref.at[pl.ds(first, count)], whole.at[pl.ds(count * k, count)], sems.at[base + k])
            for k, (ref, first) in enumerate(blocks)
        ]

    row_copies = copies(row_blocks, rows_ref, 0)
    up_copies = copies(up_blocks, upstream_ref, 8)
    mat_copies = [
        pltpu.make_async_copy(mat.at[c, 0], whole, sems.at[16 + i])
        for i, (mat, whole) in enumerate(zip(mats, (gate_ref, up_ref, down_ref)))
    ]
    for copy in row_copies + mat_copies[:2] + up_copies + mat_copies[2:]:
        copy.start()
    mine = mine_ref[...]
    blank = jnp.zeros((128 - small_ref.shape[1], 128), F32)
    for i in range(8):
        block = jnp.concatenate([small_ref[i], blank], axis=0).T
        small_rows_ref[count * i : count * (i + 1), :] = block[c * count : (c + 1) * count, :]
    for copy in row_copies + mat_copies[:2]:
        copy.wait()
    if not out_merged:
        rows_out = pltpu.make_async_copy(rows_ref, rows_out_ref, sems.at[19])
        rows_out.start()
    for copy in up_copies + mat_copies[2:]:
        copy.wait()
    block = 4 * count

    def rows_step(i, carry):
        span = pl.ds(pl.multiple_of(i * block, block), block)
        small = small_rows_ref[span, :]
        weight = jnp.sum(small * mine[0:1, :], axis=-1, keepdims=True)
        slope = jnp.sum(small * mine[1:2, :], axis=-1, keepdims=True)
        gate_pre = dot(rows_ref[span, :], gate_ref[...], ((1,), (0,)))
        up_pre = dot(rows_ref[span, :], up_ref[...], ((1,), (0,)))
        raw_grad = dot(upstream_ref[span, :], down_ref[...], ((1,), (1,)))
        sigmoid_gate = jax.nn.sigmoid(gate_pre)
        activated = gate_pre * sigmoid_gate
        hidden = (activated * up_pre).astype(BF16)
        hidden_wide = hidden.astype(F32)
        weight_grad = jnp.sum(hidden_wide * raw_grad, axis=-1, keepdims=True)
        hidden_grad = raw_grad * weight
        gate_slope = sigmoid_gate * (1.0 + gate_pre * (1.0 - sigmoid_gate))
        pre_grad_ref[span, :units] = (hidden_grad * up_pre * gate_slope).astype(BF16)
        pre_grad_ref[span, units:] = (hidden_grad * activated).astype(BF16)
        logits_grad = (small * mine[2:3, :] * (slope * weight_grad)).astype(BF16)
        logits_ref[span, :] = logits_grad
        turned_logits_ref[i] = logits_grad.astype(F32).T[:8]
        hidden_ref[span, :] = hidden
        weight_ref[span, :] = jnp.broadcast_to(weight, (block, 128))
        turned_ref[i] = (hidden_wide * weight).T.astype(BF16)
        return carry

    lax.fori_loop(0, 2, rows_step, 0)
    width = rows_ref.shape[1]
    total = 8 * count
    if out_merged:
        each = width // (2 * units)
        for i in range(each):
            part = pre_grad_ref[i * (total // each) : (i + 1) * (total // each), :]
            down_out_ref[units : units + total // each, i * 2 * units : (i + 1) * 2 * units] = part
    else:
        pre_out_ref[...] = pre_grad_ref[...]
    chunk = 512 if width % 512 == 0 else 128

    def columns_step(i, carry):
        span = pl.ds(pl.multiple_of(i * chunk, chunk), chunk)
        out = (dot(hidden_ref[...], down_ref[:, span], ((1,), (0,))) * weight_ref[:, 0:1]).astype(BF16)
        back = (
            dot(pre_grad_ref[:, :units], gate_ref[span, :], ((1,), (1,)))
            + dot(pre_grad_ref[:, units:], up_ref[span, :], ((1,), (1,)))
            + dot(logits_ref[...], router_ref[:, span], ((1,), (0,)))
        ).astype(BF16)
        for blocks, value in ((out_blocks, out), (back_blocks, back)):
            for k, (ref, first) in enumerate(blocks):
                ref[first : first + count, span] = value[count * k : count * (k + 1)]
        router_sum = dot(
            turned_logits_ref[0].astype(BF16), rows_ref[:block, span], ((1,), (0,))
        ) + dot(turned_logits_ref[1].astype(BF16), rows_ref[block:, span], ((1,), (0,)))
        if out_merged:
            high = router_sum.astype(BF16).astype(F32)
            both = jnp.concatenate([high, router_sum - high]).astype(BF16)
            down_out_ref[down_out_ref.shape[0] - 16 :, span] = both
        else:
            router_out_ref[:, span] = router_sum
        down_out_ref[:units, span] = (
            dot(turned_ref[0], upstream_ref[:block, span], ((1,), (0,)))
            + dot(turned_ref[1], upstream_ref[block:, span], ((1,), (0,)))
        ).astype(BF16)
        return carry

    lax.fori_loop(0, width // chunk, columns_step, 0)
    if not out_merged:
        rows_out.wait()


def experts_call(c, experts, count, small, mine, router_rows, pieces, mats, out_merged):
    width, units = mats[0].shape[2:]
    total = 8 * count
    full = pl.BlockSpec(memory_space=pltpu.VMEM)
    hbm = pl.BlockSpec(memory_space=pl.ANY)
    shape = lambda rows, columns: jax.ShapeDtypeStruct((rows, columns), BF16)
    near = 4 * count if out_merged else 2 * count
    results = [shape(2 * count, width)] * 2 + [shape(near, width)] * (3 if out_merged else 6)
    results.append(shape(units + total * 2 * units // width + 16 if out_merged else units, width))
    specs = [full] * len(results)
    if not out_merged:
        results += [jax.ShapeDtypeStruct((8, width), F32), shape(total, 2 * units), shape(total, width)]
        specs += [full, full, hbm]
    return pl.pallas_call(
        lambda *refs: experts_kernel(c, experts, count, len(pieces), out_merged, *refs),
        in_specs=[full] * 3 + [hbm] * (len(pieces) + 3),
        out_specs=specs,
        out_shape=results,
        scratch_shapes=[
            pltpu.VMEM((total, width), BF16),
            pltpu.VMEM((total, width), BF16),
            pltpu.VMEM((width, units), BF16),
            pltpu.VMEM((width, units), BF16),
            pltpu.VMEM((units, width), BF16),
            pltpu.VMEM((total, units), BF16),
            pltpu.VMEM((total, 2 * units), BF16),
            pltpu.VMEM((total, 128), BF16),
            pltpu.VMEM((2, units, total // 2), BF16),
            pltpu.VMEM((2, 8, total // 2), F32),
            pltpu.VMEM((total, 128), F32),
            pltpu.VMEM((total, 128), F32),
            pltpu.SemaphoreType.DMA((20,)),
        ],
        compiler_params=pltpu.CompilerParams(vmem_limit_bytes=48 * 1024 * 1024),
        cost_estimate=pl.CostEstimate(flops=COST, bytes_accessed=20_000_000, transcendentals=0),
        name=f"experts{c}",
    )(small, mine, router_rows, *pieces, *mats)


def on_device(x_in, expert_ids, out_grad, norm_gain, router, w_gate, w_up, w_down):
    experts = router.shape[3]
    count, units = out_grad.shape[2], w_gate.shape[3]
    sharers = lax.axis_size("fsdp") // experts
    lane = jnp.arange(128)
    expert = lax.axis_index("fsdp") // sharers
    mine = jnp.stack(
        [lane == expert, lane == 2 * experts + expert, lane // experts == 1] + [lane < 0] * 5
    ).astype(F32)

    normed, extras = [], []
    for c in range(2):
        picks = expert_ids[c, 0]
        lanes = jnp.arange(experts, dtype=jnp.int32)
        first_pick = (picks[:, 0:1] == lanes).astype(F32)
        second_pick = (picks[:, 1:2] == lanes).astype(F32)
        sign = first_pick - second_pick
        rows = normalize(x_in[c, 0].astype(F32), norm_gain[c, 0]).astype(BF16)
        logits = dot(rows, router[c, 0], ((1,), (0,)))
        first_weight = jax.nn.sigmoid(jnp.sum(sign * logits, axis=-1, keepdims=True))
        second_weight = 1.0 - first_weight
        weights = first_pick * first_weight + second_pick * second_weight
        slopes = first_weight * second_weight * sign
        normed.append(rows)
        extras.append(jnp.concatenate([weights.T, sign.T, slopes.T]))
    small_rows = packed(jnp.concatenate(extras, axis=1), x_in.shape[3])

    def experts_pass(c, pieces, small, out_merged):
        router_rows = jnp.pad(router[c, 0].T, ((experts, 128 - 2 * experts), (0, 0)))
        return experts_call(
            c, experts, count, small, mine, router_rows, pieces, (w_gate, w_up, w_down), out_merged
        )

    next_fwd, prev_grad = {}, {}

    def finish_out(c, way, kept, arrived):
        section_out = (x_in[c, 0].astype(F32) + kept + arrived.astype(F32)).astype(BF16)
        next_fwd[c] = shifted(section_out, way)

    def finish_back(c, way, kept, arrived):
        normed_grad = kept + arrived.astype(F32)
        inputs_wide = x_in[c, 0].astype(F32)
        _, pullback = jax.vjp(lambda values: normalize(values, norm_gain[c, 0]), inputs_wide)
        input_grad = (out_grad[c, 0].astype(F32) + pullback(normed_grad)[0]).astype(BF16)
        prev_grad[c] = shifted(input_grad, way)

    scope = jax.named_scope
    own_o1 = out_grad[1, 0]
    with scope("nO1own"):
        near_own = ring(own_o1, 1), ring(own_o1, -1)
    with scope("zO1"):
        other_o1 = across(own_o1)
    with scope("zN1"):
        pair_n1 = pair_rows(after(jnp.concatenate([normed[1], small_rows]), other_o1, *near_own), count)
    with scope("nO1other"):
        near_other = near_rows(after(other_o1, *near_own))
    with scope("fO1"):
        low, high, *_ = lax.optimization_barrier((near_own[0], near_other[1], near_own[1], near_other[0]))
        far_o1 = ring(low, 1), ring(high, -1)
    with scope("nN1"):
        near_n1 = near_rows(after(pair_n1, *near_other))
    with scope("z0"):
        pair_0 = pair_rows(after(jnp.concatenate([out_grad[0, 0], normed[0]]), pair_n1), 2 * count)
    with scope("fN1"):
        far_n1 = far_rows(near_n1, count)
    with scope("n0"):
        near_0 = near_rows(after(pair_0, *far_o1, *far_n1))
    with scope("mN"):
        mirror_rows = mirrored(after(normed[1], pair_0))
    with scope("zM"):
        pair_m = pair_rows(after(mirror_rows, *far_n1), count)
    with scope("pass1"):
        pieces_n1 = (pair_n1, *near_n1, *far_n1)
        small = unpacked(extra_rows(after(pieces_n1, pair_0), count))
        blocks_o1 = (own_o1, other_o1, near_own[0], near_other[0], near_own[1], near_other[1], *far_o1)
        *far1, own1, left1, right1, mirror1 = experts_pass(1, blocks_o1 + pieces_n1, small, True)
    with scope("s1"):
        sfar_1 = far_sums(far1)
    with scope("m1"):
        mirror_grads = mirrored(mirror1)
    with scope("f0"):
        far_0 = far_rows(after(near_0, *sfar_1), 2 * count)
    with scope("t1"):
        snear_1 = near_sums(left1, right1, sfar_1)
    with scope("pass0"):
        *far0, own_o, left_o, right_o, own_b, left_b, right_b, down0, router0, pre0, rows0 = experts_pass(
            0, (pair_0, *near_0, *far_0), small, False
        )
    with scope("s0"):
        sfar_0 = far_sums(far0)
    with scope("rz"):
        first_row = mirror_grads.shape[0] - 16
        router_terms = mirror_grads[first_row:].astype(F32)
        routers = jnp.concatenate([router0[experts:], router_terms[experts : 2 * experts] + router_terms[3 * experts :]])
        routers = routers + flipped(routers, RING)
        high = lax.reduce_precision(routers, 8, 7)
        router_rows = jnp.concatenate([high, routers - high]).astype(BF16)
    with scope("tback0"):
        snear_b = near_sums(*after((left_b, right_b), router_rows), (sfar_0[0][count:], sfar_0[1][count:]))
    with scope("z1"):
        kept_1, arrived_1 = pair_sums(own1, snear_1)
    with scope("tout0"):
        snear_o = near_sums(left_o, right_o, (sfar_0[0][:count], sfar_0[1][:count]))
    with scope("end1"):
        finish_out(1, -1, kept_1[:count], arrived_1[:count])
        finish_back(1, 1, kept_1[count:], arrived_1[count:])
    with scope("nM"):
        near_m = near_rows(after(jnp.concatenate([pair_m, router_rows]), *snear_b))
    with scope("zback0"):
        kept_b, arrived_b = pair_sums(after(own_b, arrived_1), snear_b)
    with scope("zout0"):
        kept_o, arrived_o = pair_sums(after(own_o, next_fwd[1], prev_grad[1]), snear_o)
    with scope("fM"):
        low, high = near_m[0], near_m[1][count : 2 * count]
        low = jnp.concatenate([low[:count], low[2 * count :]])
        low, high = lax.optimization_barrier((low, high))
        far_m = ring(low, 1), ring(high, -1)
    with scope("endback0"):
        finish_back(0, -1, kept_b, arrived_b)
    with scope("endout0"):
        finish_out(0, 1, kept_o, arrived_o)
    far_rows_all = all_rows((pair_m, *near_m, *far_m), count)
    router_parts = [router_rows, near_m[0][2 * count :], near_m[1][2 * count :], far_m[0][count:]]
    routers = sum(part.astype(F32) for part in router_parts)
    routers = routers[: 2 * experts] + routers[2 * experts :]

    def both(own, other):
        return (lax.reduce_precision(own, 8, 7) + lax.reduce_precision(other.astype(F32), 8, 7)).astype(BF16)

    far_pre = mirror_grads[units:first_row]
    far_pre = jnp.concatenate(jnp.split(far_pre, far_pre.shape[1] // (2 * units), axis=1))

    def weight_grad(first):
        span = slice(first, first + units)
        own = lax.optimization_barrier(dot(rows0, pre0[:, span], ((0,), (0,))).astype(BF16))
        return both(own.astype(F32), dot(far_rows_all, far_pre[:, span], ((0,), (0,))))

    grad_gate, grad_up = weight_grad(0), weight_grad(units)
    grad_down = both(down0.astype(F32), mirror_grads[:units])
    grad_router = both(routers[:experts], routers[experts:]).T
    return (
        jnp.stack([next_fwd[0], next_fwd[1]])[:, None],
        jnp.stack([prev_grad[0], prev_grad[1]])[:, None],
        grad_gate[None],
        grad_up[None],
        grad_down[None],
        grad_router[None],
    )


def solution(mesh):
    in_specs = (
        P(None, "section", "fsdp", None),
        P(None, "section", "fsdp", None),
        P(None, "section", "fsdp", None),
        P(None, "section", None),
        P(None, "section", None, None),
        P(None, "section", None, "fsdp"),
        P(None, "section", None, "fsdp"),
        P(None, "section", "fsdp", None),
    )
    out_specs = (
        P(None, "section", "fsdp", None),
        P(None, "section", "fsdp", None),
        P("section", None, "fsdp"),
        P("section", None, "fsdp"),
        P("section", "fsdp", None),
        P("section", None, None),
    )
    return jax.shard_map(
        on_device, mesh=mesh, in_specs=in_specs, out_specs=out_specs, check_vma=False
    )
```

```python
import jax
import jax.numpy as jnp
from jax import lax
from jax.experimental import pallas as pl
from jax.experimental.pallas import tpu as pltpu
from jax.sharding import PartitionSpec as P

EPSILON = 1e-05
RING = 4
BF16 = jnp.bfloat16
F32 = jnp.float32
COST = 20_000_000_000


def permuted(value, axis, target):
    pairs = [(source, target(source)) for source in range(lax.axis_size(axis))]
    return lax.ppermute(value, axis, pairs)


def shifted(value, steps):
    count = lax.axis_size("section")
    return permuted(value, "section", lambda s: (s + steps) % count)


def mirrored(value):
    count = lax.axis_size("section")
    return permuted(value, "section", lambda s: count - 1 - s)


def ring(value, steps):
    return permuted(value, "fsdp", lambda s: s // RING * RING + (s + steps) % RING)


def across(value):
    return permuted(value, "fsdp", lambda s: s ^ RING)


def flipped(value, mask):
    return permuted(value, "fsdp", lambda s: s ^ mask)


def add_half(first, second):
    return (first.astype(F32) + second.astype(F32)).astype(BF16)


def after(value, *earlier):
    return lax.optimization_barrier((value, *earlier))[0]


def pair_rows(own, count):
    other = across(own)
    parts = [own[:count], other[:count], own[count:], other[count:]]
    return jnp.concatenate(parts if own.shape[0] > count else parts[:2])


def near_rows(pair):
    return ring(pair, 1), ring(pair, -1)


def far_rows(near, count):
    def part(rows, z):
        extra = (rows.shape[0] - 2 * count) // 2
        first, second = z * count, 2 * count + z * extra
        kept = rows[first : first + count]
        return jnp.concatenate([kept, rows[second : second + extra]]) if extra else kept

    low, high = lax.optimization_barrier((part(near[0], 0), part(near[1], 1)))
    return ring(low, 1), ring(high, -1)


def all_rows(pieces, count):
    return jnp.concatenate([piece[: 2 * count] for piece in pieces[:3]] + [piece[:count] for piece in pieces[3:]])


def extra_rows(pieces, count):
    return jnp.concatenate([piece[2 * count :] for piece in pieces[:3]] + [piece[count:] for piece in pieces[3:]])


def far_sums(far):
    return ring(far[0], 1), ring(far[1], -1)


def near_sums(left, right, far):
    half = left.shape[0] // 2
    right = jnp.concatenate([add_half(right[:half], far[0]), right[half:]])
    left = jnp.concatenate([left[:half], add_half(left[half:], far[1])])
    right, left = lax.optimization_barrier((right, left))
    return ring(right, 1), ring(left, -1)


def pair_sums(own, near):
    half = own.shape[0] // 2
    total = own.astype(F32) + near[0].astype(F32) + near[1].astype(F32)
    return total[:half], across(total[half:].astype(BF16))


def packed(values, width):
    flat = jnp.pad(values.reshape(-1), (0, width - values.size))
    first = lax.reduce_precision(flat, 8, 7)
    second = lax.reduce_precision(flat - first, 8, 7)
    terms = jnp.stack([first, second, flat - first - second]).astype(BF16)
    return jnp.pad(terms, ((0, 5), (0, 0)))


def unpacked(rows):
    terms = rows.reshape(8, 8, -1).astype(F32)
    return (terms[:, 0] + terms[:, 1] + terms[:, 2]).reshape(8, -1, 128)


def normalize(values, scales):
    factor = lax.rsqrt(jnp.mean(values * values, axis=-1, keepdims=True) + EPSILON)
    return values * factor * scales


def dot(first, second, contract):
    return lax.dot_general(first, second, (contract, ((), ())), preferred_element_type=F32)


def in_places(refs, count):
    if len(refs) == 5:
        each = [(refs, 2 * count, 0), (refs, 2 * count, count)]
    else:
        each = [(refs[:-5], count, 0), (refs[-5:], count, 0)]
    result = []
    for mine, step, first in each:
        if len(mine) == 8:
            result.append([(ref, 0) for ref in mine])
        else:
            result.append([(mine[k // 2], k % 2 * step + first) for k in range(6)] + [(mine[3], first), (mine[4], first)])
    return result


def out_places(refs, count, merged):
    result = []
    for which in range(2):
        near = refs[2:5] if merged else refs[2 + 3 * which : 5 + 3 * which]
        step, first = (2 * count, which * count) if merged else (count, 0)
        far = [(refs[i], which * count) for i in range(2)]
        result.append([(near[k // 2], k % 2 * step + first) for k in range(6)] + far)
    return result


def experts_kernel(c, experts, count, taken, out_merged, *refs):
    small_ref, mine_ref, router_ref = refs[:3]
    refs = refs[3:]
    up_blocks, row_blocks = in_places(refs[:taken], count)
    mats, refs = refs[taken : taken + 3], refs[taken + 3 :]
    taken = 5 if out_merged else 8
    out_blocks, back_blocks = out_places(refs[:taken], count, out_merged)
    refs = refs[taken:]
    down_out_ref, refs = refs[0], refs[1:]
    if not out_merged:
        router_out_ref, pre_out_ref, rows_out_ref = refs[:3]
        refs = refs[3:]
    rows_ref, upstream_ref, gate_ref, up_ref, down_ref, hidden_ref, pre_grad_ref, logits_ref = refs[:8]
    turned_ref, turned_logits_ref, weight_ref, small_rows_ref, sems = refs[8:]
    units = gate_ref.shape[1]

    def copies(blocks, whole, base):
        return [
            pltpu.make_async_copy(ref.at[pl.ds(first, count)], whole.at[pl.ds(count * k, count)], sems.at[base + k])
            for k, (ref, first) in enumerate(blocks)
        ]

    row_copies = copies(row_blocks, rows_ref, 0)
    up_copies = copies(up_blocks, upstream_ref, 8)
    mat_copies = [
        pltpu.make_async_copy(mat.at[c, 0], whole, sems.at[16 + i])
        for i, (mat, whole) in enumerate(zip(mats, (gate_ref, up_ref, down_ref)))
    ]
    for copy in row_copies + mat_copies[:2] + up_copies + mat_copies[2:]:
        copy.start()
    mine = mine_ref[...]
    blank = jnp.zeros((128 - small_ref.shape[1], 128), F32)
    for i in range(8):
        block = jnp.concatenate([small_ref[i], blank], axis=0).T
        small_rows_ref[count * i : count * (i + 1), :] = block[c * count : (c + 1) * count, :]
    for copy in row_copies + mat_copies[:2]:
        copy.wait()
    if not out_merged:
        rows_out = pltpu.make_async_copy(rows_ref, rows_out_ref, sems.at[19])
        rows_out.start()
    for copy in up_copies + mat_copies[2:]:
        copy.wait()
    block = 4 * count

    def rows_step(i, carry):
        span = pl.ds(pl.multiple_of(i * block, block), block)
        small = small_rows_ref[span, :]
        weight = jnp.sum(small * mine[0:1, :], axis=-1, keepdims=True)
        slope = jnp.sum(small * mine[1:2, :], axis=-1, keepdims=True)
        gate_pre = dot(rows_ref[span, :], gate_ref[...], ((1,), (0,)))
        up_pre = dot(rows_ref[span, :], up_ref[...], ((1,), (0,)))
        raw_grad = dot(upstream_ref[span, :], down_ref[...], ((1,), (1,)))
        sigmoid_gate = jax.nn.sigmoid(gate_pre)
        activated = gate_pre * sigmoid_gate
        hidden = (activated * up_pre).astype(BF16)
        hidden_wide = hidden.astype(F32)
        weight_grad = jnp.sum(hidden_wide * raw_grad, axis=-1, keepdims=True)
        hidden_grad = raw_grad * weight
        gate_slope = sigmoid_gate * (1.0 + gate_pre * (1.0 - sigmoid_gate))
        pre_grad_ref[span, :units] = (hidden_grad * up_pre * gate_slope).astype(BF16)
        pre_grad_ref[span, units:] = (hidden_grad * activated).astype(BF16)
        logits_grad = (small * mine[2:3, :] * (slope * weight_grad)).astype(BF16)
        logits_ref[span, :] = logits_grad
        turned_logits_ref[i] = logits_grad.astype(F32).T[:8]
        hidden_ref[span, :] = hidden
        weight_ref[span, :] = jnp.broadcast_to(weight, (block, 128))
        turned_ref[i] = (hidden_wide * weight).T.astype(BF16)
        return carry

    lax.fori_loop(0, 2, rows_step, 0)
    width = rows_ref.shape[1]
    total = 8 * count
    if out_merged:
        each = width // (2 * units)
        for i in range(each):
            part = pre_grad_ref[i * (total // each) : (i + 1) * (total // each), :]
            down_out_ref[units : units + total // each, i * 2 * units : (i + 1) * 2 * units] = part
    else:
        pre_out_ref[...] = pre_grad_ref[...]
    chunk = 512 if width % 512 == 0 else 128

    def columns_step(i, carry):
        span = pl.ds(pl.multiple_of(i * chunk, chunk), chunk)
        out = (dot(hidden_ref[...], down_ref[:, span], ((1,), (0,))) * weight_ref[:, 0:1]).astype(BF16)
        back = (
            dot(pre_grad_ref[:, :units], gate_ref[span, :], ((1,), (1,)))
            + dot(pre_grad_ref[:, units:], up_ref[span, :], ((1,), (1,)))
            + dot(logits_ref[...], router_ref[:, span], ((1,), (0,)))
        ).astype(BF16)
        for blocks, value in ((out_blocks, out), (back_blocks, back)):
            for k, (ref, first) in enumerate(blocks):
                ref[first : first + count, span] = value[count * k : count * (k + 1)]
        router_sum = dot(
            turned_logits_ref[0].astype(BF16), rows_ref[:block, span], ((1,), (0,))
        ) + dot(turned_logits_ref[1].astype(BF16), rows_ref[block:, span], ((1,), (0,)))
        if out_merged:
            high = router_sum.astype(BF16).astype(F32)
            both = jnp.concatenate([high, router_sum - high]).astype(BF16)
            down_out_ref[down_out_ref.shape[0] - 16 :, span] = both
        else:
            router_out_ref[:, span] = router_sum
        down_out_ref[:units, span] = (
            dot(turned_ref[0], upstream_ref[:block, span], ((1,), (0,)))
            + dot(turned_ref[1], upstream_ref[block:, span], ((1,), (0,)))
        ).astype(BF16)
        return carry

    lax.fori_loop(0, width // chunk, columns_step, 0)
    if not out_merged:
        rows_out.wait()


def experts_call(c, experts, count, small, mine, router_rows, pieces, mats, out_merged):
    width, units = mats[0].shape[2:]
    total = 8 * count
    full = pl.BlockSpec(memory_space=pltpu.VMEM)
    hbm = pl.BlockSpec(memory_space=pl.ANY)
    shape = lambda rows, columns: jax.ShapeDtypeStruct((rows, columns), BF16)
    near = 4 * count if out_merged else 2 * count
    results = [shape(2 * count, width)] * 2 + [shape(near, width)] * (3 if out_merged else 6)
    results.append(shape(units + total * 2 * units // width + 16 if out_merged else units, width))
    specs = [full] * len(results)
    if not out_merged:
        results += [jax.ShapeDtypeStruct((8, width), F32), shape(total, 2 * units), shape(total, width)]
        specs += [full, full, hbm]
    return pl.pallas_call(
        lambda *refs: experts_kernel(c, experts, count, len(pieces), out_merged, *refs),
        in_specs=[full] * 3 + [hbm] * (len(pieces) + 3),
        out_specs=specs,
        out_shape=results,
        scratch_shapes=[
            pltpu.VMEM((total, width), BF16),
            pltpu.VMEM((total, width), BF16),
            pltpu.VMEM((width, units), BF16),
            pltpu.VMEM((width, units), BF16),
            pltpu.VMEM((units, width), BF16),
            pltpu.VMEM((total, units), BF16),
            pltpu.VMEM((total, 2 * units), BF16),
            pltpu.VMEM((total, 128), BF16),
            pltpu.VMEM((2, units, total // 2), BF16),
            pltpu.VMEM((2, 8, total // 2), F32),
            pltpu.VMEM((total, 128), F32),
            pltpu.VMEM((total, 128), F32),
            pltpu.SemaphoreType.DMA((20,)),
        ],
        compiler_params=pltpu.CompilerParams(vmem_limit_bytes=48 * 1024 * 1024),
        cost_estimate=pl.CostEstimate(flops=COST, bytes_accessed=20_000_000, transcendentals=0),
        name=f"experts{c}",
    )(small, mine, router_rows, *pieces, *mats)


def on_device(x_in, expert_ids, out_grad, norm_gain, router, w_gate, w_up, w_down):
    experts = router.shape[3]
    count, units = out_grad.shape[2], w_gate.shape[3]
    sharers = lax.axis_size("fsdp") // experts
    lane = jnp.arange(128)
    expert = lax.axis_index("fsdp") // sharers
    mine = jnp.stack(
        [lane == expert, lane == 2 * experts + expert, lane // experts == 1] + [lane < 0] * 5
    ).astype(F32)

    normed, extras = [], []
    for c in range(2):
        picks = expert_ids[c, 0]
        lanes = jnp.arange(experts, dtype=jnp.int32)
        first_pick = (picks[:, 0:1] == lanes).astype(F32)
        second_pick = (picks[:, 1:2] == lanes).astype(F32)
        sign = first_pick - second_pick
        rows = normalize(x_in[c, 0].astype(F32), norm_gain[c, 0]).astype(BF16)
        logits = dot(rows, router[c, 0], ((1,), (0,)))
        first_weight = jax.nn.sigmoid(jnp.sum(sign * logits, axis=-1, keepdims=True))
        second_weight = 1.0 - first_weight
        weights = first_pick * first_weight + second_pick * second_weight
        slopes = first_weight * second_weight * sign
        normed.append(rows)
        extras.append(jnp.concatenate([weights.T, sign.T, slopes.T]))
    small_rows = packed(jnp.concatenate(extras, axis=1), x_in.shape[3])

    def experts_pass(c, pieces, small, out_merged):
        router_rows = jnp.pad(router[c, 0].T, ((experts, 128 - 2 * experts), (0, 0)))
        return experts_call(
            c, experts, count, small, mine, router_rows, pieces, (w_gate, w_up, w_down), out_merged
        )

    next_fwd, prev_grad = {}, {}

    def finish_out(c, way, kept, arrived):
        section_out = (x_in[c, 0].astype(F32) + kept + arrived.astype(F32)).astype(BF16)
        next_fwd[c] = shifted(section_out, way)

    def finish_back(c, way, kept, arrived):
        normed_grad = kept + arrived.astype(F32)
        inputs_wide = x_in[c, 0].astype(F32)
        _, pullback = jax.vjp(lambda values: normalize(values, norm_gain[c, 0]), inputs_wide)
        input_grad = (out_grad[c, 0].astype(F32) + pullback(normed_grad)[0]).astype(BF16)
        prev_grad[c] = shifted(input_grad, way)

    scope = jax.named_scope
    own_o1 = out_grad[1, 0]
    with scope("nO1own"):
        near_own = ring(own_o1, 1), ring(own_o1, -1)
    with scope("zO1"):
        other_o1 = across(own_o1)
    with scope("zN1"):
        pair_n1 = pair_rows(after(jnp.concatenate([normed[1], small_rows]), other_o1, *near_own), count)
    with scope("nO1other"):
        near_other = near_rows(after(other_o1, *near_own))
    with scope("fO1"):
        low, high, *_ = lax.optimization_barrier((near_own[0], near_other[1], near_own[1], near_other[0]))
        far_o1 = ring(low, 1), ring(high, -1)
    with scope("nN1"):
        near_n1 = near_rows(after(pair_n1, *near_other))
    with scope("z0"):
        pair_0 = pair_rows(after(jnp.concatenate([out_grad[0, 0], normed[0]]), pair_n1), 2 * count)
    with scope("fN1"):
        far_n1 = far_rows(near_n1, count)
    with scope("n0"):
        near_0 = near_rows(after(pair_0, *far_o1, *far_n1))
    with scope("mN"):
        mirror_rows = mirrored(after(normed[1], pair_0))
    with scope("zM"):
        pair_m = pair_rows(after(mirror_rows, *far_n1), count)
    with scope("pass1"):
        pieces_n1 = (pair_n1, *near_n1, *far_n1)
        small = unpacked(extra_rows(after(pieces_n1, pair_0), count))
        blocks_o1 = (own_o1, other_o1, near_own[0], near_other[0], near_own[1], near_other[1], *far_o1)
        *far1, own1, left1, right1, mirror1 = experts_pass(1, blocks_o1 + pieces_n1, small, True)
    with scope("s1"):
        sfar_1 = far_sums(far1)
    with scope("m1"):
        mirror_grads = mirrored(mirror1)
    with scope("f0"):
        far_0 = far_rows(after(near_0, *sfar_1), 2 * count)
    with scope("t1"):
        snear_1 = near_sums(left1, right1, sfar_1)
    with scope("pass0"):
        *far0, own_o, left_o, right_o, own_b, left_b, right_b, down0, router0, pre0, rows0 = experts_pass(
            0, (pair_0, *near_0, *far_0), small, False
        )
    with scope("s0"):
        sfar_0 = far_sums(far0)
    with scope("rz"):
        first_row = mirror_grads.shape[0] - 16
        router_terms = mirror_grads[first_row:].astype(F32)
        routers = jnp.concatenate([router0[experts:], router_terms[experts : 2 * experts] + router_terms[3 * experts :]])
        routers = routers + flipped(routers, RING)
        high = lax.reduce_precision(routers, 8, 7)
        router_rows = jnp.concatenate([high, routers - high]).astype(BF16)
    with scope("tback0"):
        snear_b = near_sums(*after((left_b, right_b), router_rows), (sfar_0[0][count:], sfar_0[1][count:]))
    with scope("z1"):
        kept_1, arrived_1 = pair_sums(own1, snear_1)
    with scope("tout0"):
        snear_o = near_sums(left_o, right_o, (sfar_0[0][:count], sfar_0[1][:count]))
    with scope("end1"):
        finish_out(1, -1, kept_1[:count], arrived_1[:count])
        finish_back(1, 1, kept_1[count:], arrived_1[count:])
    with scope("nM"):
        near_m = near_rows(after(jnp.concatenate([pair_m, router_rows]), *snear_b))
    with scope("zback0"):
        kept_b, arrived_b = pair_sums(after(own_b, arrived_1), snear_b)
    with scope("zout0"):
        kept_o, arrived_o = pair_sums(after(own_o, next_fwd[1], prev_grad[1]), snear_o)
    with scope("fM"):
        low, high = near_m[0], near_m[1][count : 2 * count]
        low = jnp.concatenate([low[:count], low[2 * count :]])
        low, high = lax.optimization_barrier((low, high))
        far_m = ring(low, 1), ring(high, -1)
    with scope("endback0"):
        finish_back(0, -1, kept_b, after(arrived_b, *near_m))
    with scope("endout0"):
        finish_out(0, 1, kept_o, arrived_o)
    far_rows_all = all_rows((pair_m, *near_m, *far_m), count)
    router_parts = [router_rows, near_m[0][2 * count :], near_m[1][2 * count :], far_m[0][count:]]
    routers = sum(part.astype(F32) for part in router_parts)
    routers = routers[: 2 * experts] + routers[2 * experts :]

    def both(own, other):
        return (lax.reduce_precision(own, 8, 7) + lax.reduce_precision(other.astype(F32), 8, 7)).astype(BF16)

    far_pre = mirror_grads[units:first_row]
    far_pre = jnp.concatenate(jnp.split(far_pre, far_pre.shape[1] // (2 * units), axis=1))

    def weight_grad(first):
        span = slice(first, first + units)
        own = lax.optimization_barrier(dot(rows0, pre0[:, span], ((0,), (0,))).astype(BF16))
        return both(own.astype(F32), dot(far_rows_all, far_pre[:, span], ((0,), (0,))))

    grad_gate, grad_up = weight_grad(0), weight_grad(units)
    grad_down = both(down0.astype(F32), mirror_grads[:units])
    grad_router = both(routers[:experts], routers[experts:]).T
    return (
        jnp.stack([next_fwd[0], next_fwd[1]])[:, None],
        jnp.stack([prev_grad[0], prev_grad[1]])[:, None],
        grad_gate[None],
        grad_up[None],
        grad_down[None],
        grad_router[None],
    )


def solution(mesh):
    in_specs = (
        P(None, "section", "fsdp", None),
        P(None, "section", "fsdp", None),
        P(None, "section", "fsdp", None),
        P(None, "section", None),
        P(None, "section", None, None),
        P(None, "section", None, "fsdp"),
        P(None, "section", None, "fsdp"),
        P(None, "section", "fsdp", None),
    )
    out_specs = (
        P(None, "section", "fsdp", None),
        P(None, "section", "fsdp", None),
        P("section", None, "fsdp"),
        P("section", None, "fsdp"),
        P("section", "fsdp", None),
        P("section", None, None),
    )
    return jax.shard_map(
        on_device, mesh=mesh, in_specs=in_specs, out_specs=out_specs, check_vma=False
    )
```
